32 devices in a mesh: ccd: 8 (over z, x), tile: 4 (over y, core).
Axes of the slice: x: 2, y: 2, z: 4, core: 2. Of those that a mesh axis runs over, the one named last changes fastest.
Arguments:
- visit_image: bfloat16 [4096, 1024], P(('ccd', 'tile')), may hold values from -6 to 6
- mask_bits: int32 [4096, 1024], P(('ccd', 'tile')), may hold values from 0 to 15
- visit_weight: float32 [8], P('ccd'), may hold values from 1 to 4
- basis_cols: bfloat16 [31, 21], replicated, may hold values from -1.25 to 1.25
- basis_rows: bfloat16 [31, 21], replicated, may hold values from -1.25 to 1.25
- kernel_coef: float32 [8, 31, 6], P('ccd'), may hold values from -1 to 1
- row_warp: bfloat16 [4096, 512], P(('ccd', 'tile')), may hold values from -1 to 1, as said below
- col_warp: bfloat16 [8, 1024, 1024], P('ccd'), may hold values from -1 to 1, as said below
- dest_owner: int32 [2048, 1], P(('ccd', 'tile')), may hold values from 0 to 7; in each aligned block of 64 rows (0 to 63, 64 to 127, ...) at most 16 rows name the same one
- dest_block: int32 [2048], P(('ccd', 'tile')), may hold values from 0 to 63
- new_science: float32 [4096, 1024], P(('ccd', 'tile')), may hold values from -6 to 6
- tmpl_owner: int32 [2048, 1], P(('ccd', 'tile')), may hold values from 0 to 7; in each aligned block of 64 rows (0 to 63, 64 to 127, ...) at most 16 rows name the same one
- tmpl_block: int32 [2048], P(('ccd', 'tile')), may hold values from 0 to 63
Outputs:
- coadd: float32 [4096, 1024], P(('ccd', 'tile'))
- difference: float32 [4096, 1024], P(('ccd', 'tile'))
The draws below stay inside these ranges and needn't reach their ends.
Inputs may be any that keep to these rules, and one draw needn't show every extreme that they name: `dest_owner`: within the 64 rows of one device no patch is named more than 16 times, a bound that some block reaches. `tmpl_owner`: within the 64 rows of one device no patch is named more than 16 times, a bound that some block reaches. `row_warp`: Lanczos-3 interpolation weights for a dither of 0 or plus or minus 512 / 2 rows plus a shift within 8 pixels, and a scale change within 3 / 512; rows that fall off the cutout are zero. `col_warp`: Lanczos-3 interpolation weights for a shift within 8 pixels and a scale change within 3 / 1024; every nonzero lies within 14 of the diagonal.
All inputs are finite; a program needn't handle non-finite values.
Results may differ from the reference program's by a relative error of at most 0.015.
Values may be sent and summed in bfloat16 or wider, within the bound.
A program may use at most 192 MiB of HBM per device.

```python
import math
import jax
import jax.numpy as jnp
import numpy as np
from jax import lax

W = 1024
ROWS_DEV = 128
NB = 31
KT = 21
NPOLY = 6
BLOCK_ROWS = 16
BLOCK_COLUMNS = 128
CH = 512
ROWS = 4096
NBLK = 64
CAP = 16
ALLBLK = 2048
N_CCD = 8
N_TILE = 4


def lanczos_weight(offset):
    inside = jnp.abs(offset) < 3.0
    return jnp.where(inside, jnp.sinc(offset) * jnp.sinc(offset / 3.0), 0.0)


def draw_row_warp(key, part):
    key_shift, key_scale, key_dither = jax.random.split(jax.random.fold_in(key, 11), 3)
    shift = jax.random.uniform(key_shift, (N_CCD, 1, 1), jnp.float32, -8.0, 8.0)
    dither = jax.random.randint(key_dither, (N_CCD,), -1, 2)
    dither = jnp.where(jnp.arange(N_CCD) == 0, 1, dither).astype(jnp.float32)
    shift = shift + (dither * (CH // 2)).reshape(N_CCD, 1, 1)
    scale = jax.random.uniform(key_scale, (N_CCD, 1, 1), jnp.float32, -3.0 / CH, 3.0 / CH)
    outs = jnp.arange(CH, dtype=jnp.float32)[None, :, None]
    ins = jnp.arange(CH, dtype=jnp.float32)[None, None, :]
    mats = lanczos_weight(ins - (outs * (1.0 + scale) + shift))
    return mats.reshape(N_CCD * CH, CH).astype(jnp.bfloat16)


def draw_col_warp(key, part):
    key_shift, key_scale = jax.random.split(jax.random.fold_in(key, 23))
    shift = jax.random.uniform(key_shift, (N_CCD, 1, 1), jnp.float32, -8.0, 8.0)
    scale = jax.random.uniform(key_scale, (N_CCD, 1, 1), jnp.float32, -3.0 / W, 3.0 / W)
    ins = jnp.arange(W, dtype=jnp.float32)[None, :, None]
    outs = jnp.arange(W, dtype=jnp.float32)[None, None, :]
    mats = lanczos_weight(ins - (outs * (1.0 + scale) + shift))
    return mats.astype(jnp.bfloat16)


def touch_ends(drawn, own_key, least, high):
    index_at = [jax.random.randint(jax.random.fold_in(own_key, axis), (), 0, length) for axis, length in enumerate(drawn.shape)]
    main_axis = drawn.shape.index(max(drawn.shape))
    beside = index_at[:main_axis] + [(index_at[main_axis] + 1) % drawn.shape[main_axis]] + index_at[main_axis + 1:]
    return drawn.at[tuple(index_at)].set(least).at[tuple(beside)].set(high)


def levels(own_key, dims, pieces, smallest, largest):
    def one(dim, shards_of):
        heights = jax.random.uniform(jax.random.fold_in(jax.random.fold_in(own_key, 6), dim), (shards_of,), jnp.float32, smallest / len(pieces), largest / len(pieces))
        return jnp.repeat(jnp.exp(heights), dims[dim] // shards_of).reshape((-1,) + (1,) * (len(dims) - dim - 1))

    gain = one(*pieces[0])
    for cut in pieces[1:]:
        gain = gain * one(*cut)
    return gain


def deal_out(key, own, number, rows, amount, top, bound, slope):
    order = jax.random.permutation(key, amount)
    crowded, usual = shares(amount, rows * top, bound, slope, True), shares(amount, rows * top, bound, slope, False)
    places = jnp.arange(amount)

    def named(lengths, turn):
        used = int((lengths > 0).sum())
        fixed = max(1, used // 4)
        moved = fixed + (places - fixed + turn * (used - fixed)) % max(1, amount - fixed)
        return jnp.zeros((amount,), jnp.int32).at[order[jnp.where(places < fixed, places, moved)]].set(jnp.asarray(lengths, jnp.int32))

    lengths = jnp.where(number % 4 == 0, named(crowded, number // 4), named(usual, number - number // 4 - 1))
    mixed = jax.random.permutation(jax.random.fold_in(own, 3), amount)
    source_of, receiver = mixed[0:amount // 2 * 2:2], mixed[1:amount // 2 * 2:2]
    margin = jnp.minimum(lengths[source_of] - 1, bound - lengths[receiver]) // 2
    margin = jnp.where((source_of == order[0]) | (receiver == order[0]) | (lengths[receiver] == 0), 0, jnp.maximum(margin, 0))
    moved = jax.random.randint(jax.random.fold_in(own, 4), (amount // 2,), 0, 1 << 20) % (margin + 1)
    lengths = lengths.at[source_of].add(-moved).at[receiver].add(moved)
    members = jnp.searchsorted(jnp.cumsum(lengths), jnp.arange(rows * top), side="right").astype(jnp.int32)
    grid = members.reshape(top, rows).T
    grid = grid[jax.random.permutation(jax.random.fold_in(own, 1), rows)]
    turn = jax.random.randint(jax.random.fold_in(own, 2), (rows, 1), 0, top)
    return jnp.take_along_axis(grid, (jnp.arange(top)[None, :] + turn) % top, axis=1)


def shares(amount, total, limit, slope, full):
    portions = [(1 << 20) // math.isqrt(rank ** slope) + 1 for rank in range(1, amount + 1)]
    largest = limit if full else min(limit, max(-(-total // amount), total * portions[0] // sum(portions)))
    least = 1 if total - largest >= amount - 1 else 0
    given, spare = [largest] + [least] * (amount - 1), total - largest - least * (amount - 1)
    while spare > 0:
        free = [i for i in range(1, amount) if given[i] < largest] or [i for i in range(1, amount) if given[i] < limit]
        whole, left = sum([portions[i] for i in free]), spare
        for i in free:
            more = min(limit - given[i], max(1, left * portions[i] // whole), spare)
            given[i] = given[i] + more
            spare = spare - more
    return np.array(given)


def centred(rng, extent, scale, reach, pieces=(), held_as=jnp.bfloat16):
    array = jax.random.normal(rng, extent, jnp.float32) * scale
    if len(pieces) > 0:
        array = levels(rng, extent, pieces, -0.22, 0.18) * array
    return jnp.clip(array, min=-reach, max=reach).astype(held_as)


def setup_inputs(seed: int = 0) -> dict:
    seeds = jax.random.split(jax.random.key(seed), 14)
    visit_image = centred(seeds[0], (ROWS, W), 1.0, 6.0, ((0, 32),))
    mask_bits = touch_ends(jax.random.randint(seeds[1], (ROWS, W), 0, 16), jax.random.fold_in(seeds[1], 1), 0, 15).astype(jnp.int32)
    visit_weight = jnp.clip(jnp.exp(math.log(4.0) - 1.3862944 * jax.random.uniform(seeds[2], (N_CCD,), jnp.float32) ** levels(seeds[2], (N_CCD,), ((0, 8),), -0.2, 0.2)), 1.0, 4.0)
    basis_cols = centred(seeds[3], (NB, KT), KT ** -0.5, 1.25)
    basis_rows = centred(seeds[4], (NB, KT), KT ** -0.5, 1.25)
    kernel_coef = centred(seeds[5], (N_CCD, NB, NPOLY), NB ** -0.5, 1.0, ((0, 8),), jnp.float32)
    row_warp = draw_row_warp(jax.random.fold_in(seeds[13], 71), 0)
    col_warp = draw_col_warp(jax.random.fold_in(seeds[13], 71), 0)
    dest_owner_keys = jax.random.split(jax.random.fold_in(seeds[8], 1), ALLBLK // NBLK)
    dest_owner_turns = jax.random.permutation(jax.random.fold_in(seeds[8], 3), ALLBLK // NBLK)
    dest_owner = jax.vmap(lambda own, number: deal_out(jax.random.fold_in(seeds[8], 2), own, number, NBLK, N_CCD, 1, CAP, 2))(dest_owner_keys, dest_owner_turns).reshape((ALLBLK, 1))
    dest_block = touch_ends(jax.random.randint(seeds[9], (ALLBLK,), 0, NBLK), jax.random.fold_in(seeds[9], 1), 0, NBLK - 1).astype(jnp.int32)
    new_science = centred(seeds[10], (ROWS, W), 1.0, 6.0, ((0, 32),), jnp.float32)
    tmpl_owner_keys = jax.random.split(jax.random.fold_in(seeds[11], 1), ALLBLK // NBLK)
    tmpl_owner_turns = jax.random.permutation(jax.random.fold_in(seeds[11], 3), ALLBLK // NBLK)
    tmpl_owner = jax.vmap(lambda own, number: deal_out(jax.random.fold_in(seeds[11], 2), own, number, NBLK, N_CCD, 1, CAP, 2))(tmpl_owner_keys, tmpl_owner_turns).reshape((ALLBLK, 1))
    tmpl_block = touch_ends(jax.random.randint(seeds[12], (ALLBLK,), 0, NBLK), jax.random.fold_in(seeds[12], 1), 0, NBLK - 1).astype(jnp.int32)
    return dict(visit_image=visit_image, mask_bits=mask_bits, visit_weight=visit_weight, basis_cols=basis_cols, basis_rows=basis_rows, kernel_coef=kernel_coef, row_warp=row_warp, col_warp=col_warp, dest_owner=dest_owner, dest_block=dest_block, new_science=new_science, tmpl_owner=tmpl_owner, tmpl_block=tmpl_block)


FLOOR = 1.0


def poly_planes(nrows, width):
    ys = (2.0 * jnp.arange(nrows, dtype=jnp.float32) + 1.0) / nrows - 1.0
    xs = (2.0 * jnp.arange(width, dtype=jnp.float32) + 1.0) / width - 1.0
    yy = ys[:, None] + jnp.zeros((1, width), jnp.float32)
    xx = xs[None, :] + jnp.zeros((nrows, 1), jnp.float32)
    return jnp.stack([jnp.ones_like(yy), yy, xx, yy * yy, yy * xx, xx * xx])


def convolve_ccd(image, coef, basis_cols, basis_rows):
    half = (KT - 1) // 2
    ext = jnp.pad(image.astype(jnp.float32), ((half, half), (0, 0)))
    colsf = basis_cols.astype(jnp.float32)
    rowsf = basis_rows.astype(jnp.float32)
    vert = jnp.zeros((NB, CH, W), jnp.float32)
    for j in range(KT):
        vert = vert + colsf[:, j, None, None] * ext[None, j:j + CH, :]
    vert = lax.optimization_barrier(vert.astype(jnp.bfloat16)).astype(jnp.float32)
    padded = jnp.pad(vert, ((0, 0), (0, 0), (half, half)))
    horiz = jnp.zeros((NB, CH, W), jnp.float32)
    for i in range(KT):
        horiz = horiz + rowsf[:, i, None, None] * padded[:, :, i:i + W]
    mixed = jnp.einsum("bp,brx->prx", coef, horiz, precision=lax.Precision.HIGHEST)
    return jnp.sum(mixed * poly_planes(CH, W), axis=0)


def reference(visit_image, mask_bits, visit_weight, basis_cols, basis_rows, kernel_coef, row_warp, col_warp, dest_owner, dest_block, new_science, tmpl_owner, tmpl_block):
    images = visit_image.reshape(N_CCD, CH, W)
    masks = mask_bits.reshape(N_CCD, CH, W)
    rowmats = row_warp.reshape(N_CCD, CH, CH)

    def per_ccd(items):
        image, mask, weight, coef, rowmat, colmat = items
        conv = convolve_ccd(image, coef, basis_cols, basis_rows)
        bad = jnp.bitwise_and(mask, 3) == 3
        wplane = jnp.where(bad, jnp.zeros_like(conv), weight + jnp.zeros_like(conv)).astype(jnp.bfloat16)
        flux = (wplane.astype(jnp.float32) * conv).astype(jnp.bfloat16)
        planes = jnp.stack([flux, wplane]).astype(jnp.float32)
        rowed = jnp.einsum("rs,psx->prx", rowmat.astype(jnp.float32), planes, precision=lax.Precision.HIGHEST)
        rowed = lax.optimization_barrier(rowed.astype(jnp.bfloat16)).astype(jnp.float32)
        return jnp.einsum("prx,xy->pry", rowed, colmat.astype(jnp.float32), precision=lax.Precision.HIGHEST)

    warped = lax.map(per_ccd, (images, masks, visit_weight, kernel_coef, rowmats, col_warp))
    blocks = warped.reshape(N_CCD, 2, N_TILE, ROWS_DEV // BLOCK_ROWS, BLOCK_ROWS, W // BLOCK_COLUMNS, BLOCK_COLUMNS)
    blocks = blocks.transpose(0, 2, 3, 5, 1, 4, 6).reshape(N_CCD, N_TILE, NBLK, 2, BLOCK_ROWS, BLOCK_COLUMNS)
    owners = dest_owner.reshape(N_CCD, N_TILE, NBLK).astype(jnp.int32)
    targets = dest_block.reshape(N_CCD, N_TILE, NBLK).astype(jnp.int32)
    tiles = (jnp.zeros((N_CCD, N_TILE, NBLK), jnp.int32) + jnp.arange(N_TILE, dtype=jnp.int32)[None, :, None])
    acc = jnp.zeros((N_CCD, N_TILE, NBLK, 2, BLOCK_ROWS, BLOCK_COLUMNS), jnp.float32).at[owners, tiles, targets].add(blocks)
    coadd_blocks = acc[:, :, :, 0] / jnp.maximum(acc[:, :, :, 1], FLOOR)
    coadd = coadd_blocks.reshape(N_CCD, N_TILE, ROWS_DEV // BLOCK_ROWS, W // BLOCK_COLUMNS, BLOCK_ROWS, BLOCK_COLUMNS).transpose(0, 1, 2, 4, 3, 5).reshape(ROWS, W)
    towners = tmpl_owner.reshape(N_CCD, N_TILE, NBLK).astype(jnp.int32)
    tblocks = tmpl_block.reshape(N_CCD, N_TILE, NBLK).astype(jnp.int32)
    template = coadd_blocks[towners, tiles, tblocks]
    template = template.reshape(N_CCD, N_TILE, ROWS_DEV // BLOCK_ROWS, W // BLOCK_COLUMNS, BLOCK_ROWS, BLOCK_COLUMNS).transpose(0, 1, 2, 4, 3, 5).reshape(ROWS, W)
    return coadd, new_science - template
```

```python
import functools

import jax
import jax.numpy as jnp
from jax import lax
from jax.experimental import pallas as pl
from jax.experimental.pallas import tpu as pltpu
from jax.sharding import PartitionSpec as P

BLOCK_ROWS = 16
BLOCK_COLUMNS = 128
FLOOR = 1.0
HALO = 16
SPAN = 256
STEP = 208
GROUP = 4


def conv_kernel(
    ntaps, cutout_rows, coef_ref, weight_ref, top_ref, image_ref, bottom_ref, mask_ref,
    cols_ref, rows_ref, flux_ref, ext_ref, acc_ref,
):
    nrows, width = image_ref.shape
    half = (ntaps - 1) // 2
    nwin = -(-width // STEP)
    nbasis = cols_ref.shape[0]
    left = 128
    ext = jnp.concatenate([top_ref[...], image_ref[...], bottom_ref[...]], axis=0).astype(jnp.float32)
    high = ext.shape[0]
    ext = jnp.concatenate(
        [jnp.zeros((high, left), jnp.float32), ext, jnp.zeros((high, 3 * 128), jnp.float32)], axis=1
    )
    ext_ref[...] = jnp.zeros_like(ext_ref)
    for k in range(nwin):
        start = STEP * k - half + left
        base = start // 128 * 128
        piece = ext[:, base : base + SPAN + 128]
        shift = start - base
        if shift:
            piece = pltpu.roll(piece, SPAN + 128 - shift, 1)
        ext_ref[0:high, k * SPAN : (k + 1) * SPAN] = piece[:, :SPAN].astype(jnp.bfloat16)
    first_row = lax.axis_index("tile") * nrows
    row = (first_row + lax.broadcasted_iota(jnp.int32, (nrows, SPAN), 0)).astype(jnp.float32)
    yn = (2.0 * row + 1.0) / cutout_rows - 1.0
    yy = yn * yn
    lane = lax.broadcasted_iota(jnp.int32, (1, SPAN), 1).astype(jnp.float32)
    acc_ref[...] = jnp.zeros_like(acc_ref)

    def one(b):
        taps = jnp.broadcast_to(cols_ref[pl.ds(b, 1), :], (nrows, SPAN))
        vtab = pltpu.roll(taps, 0, 1, stride=1, stride_axis=0).astype(jnp.bfloat16)
        taps = jnp.broadcast_to(rows_ref[pl.ds(b, 1), :], (SPAN, SPAN))
        htab = pltpu.roll(taps, 0, 1, stride=1, stride_axis=0).astype(jnp.bfloat16)
        vert = jnp.dot(vtab, ext_ref[...], preferred_element_type=jnp.float32).astype(jnp.bfloat16)
        c = [coef_ref[b, p] for p in range(6)]
        yyc = yy * c[3]
        stacked = jnp.concatenate([vert[:, k * SPAN : (k + 1) * SPAN] for k in range(nwin)], axis=0)
        horiz = jnp.dot(stacked, htab, preferred_element_type=jnp.float32)
        out = []
        for k in range(nwin):
            xn = (2.0 * (lane + float(STEP * k)) + 1.0) / width - 1.0
            even = c[0] + xn * (c[2] + xn * c[5])
            slope = c[1] + xn * c[4]
            out.append((yyc + even + yn * slope) * horiz[k * nrows : (k + 1) * nrows])
        return out

    def body(g, carry):
        total = one(g * GROUP)
        for u in range(1, GROUP):
            total = [a + b for a, b in zip(total, one(g * GROUP + u))]
        for k in range(nwin):
            acc_ref[k] += total[k]
        return carry

    lax.fori_loop(0, nbasis // GROUP, body, 0)
    conv = jnp.concatenate([acc_ref[k][:, :STEP] for k in range(nwin)], axis=1)[:, :width]
    bad = jnp.bitwise_and(mask_ref[...], 3) == 3
    plane = jnp.where(bad, 0.0, weight_ref[0]).astype(jnp.bfloat16).astype(jnp.float32)
    flux_ref[...] = (plane * conv).astype(jnp.bfloat16)


def convolve(image, top, bottom, mask, weight, coef, basis_cols, basis_rows, cutout_rows):
    nrows, width = image.shape
    nb, ntaps = basis_cols.shape
    half = (ntaps - 1) // 2
    padb = -nb % GROUP
    nwin = -(-width // STEP)
    cols = jnp.pad(
        basis_cols.astype(jnp.float32),
        ((0, padb), (HALO - half, SPAN - ntaps - (HALO - half))),
    )
    rows = basis_rows.astype(jnp.float32)
    rows = jnp.concatenate(
        [rows[:, :1], jnp.zeros((nb, SPAN - ntaps), jnp.float32), rows[:, :0:-1]], axis=1
    )
    rows = jnp.pad(rows, ((0, padb), (0, 0)))
    coef = jnp.pad(coef, ((0, padb), (0, 0)))
    smem = pl.BlockSpec(memory_space=pltpu.SMEM)
    vmem = pl.BlockSpec(memory_space=pltpu.VMEM)
    return pl.pallas_call(
        functools.partial(conv_kernel, ntaps, cutout_rows),
        out_shape=jax.ShapeDtypeStruct((nrows, width), jnp.bfloat16),
        in_specs=[smem, smem] + [vmem] * 6,
        out_specs=vmem,
        scratch_shapes=[
            pltpu.VMEM((SPAN, nwin * SPAN), jnp.bfloat16),
            pltpu.VMEM((nwin, nrows, SPAN), jnp.float32),
        ],
        compiler_params=pltpu.CompilerParams(vmem_limit_bytes=40 << 20),
        cost_estimate=pl.CostEstimate(flops=10 * 10**9, bytes_accessed=2 << 20, transcendentals=0),
        name="conv_flux",
    )(coef, weight, top, image, bottom, mask, cols, rows)


def slot_of(owners, count, capacity):
    hits = (owners[..., :, None] == jnp.arange(count)).astype(jnp.int32)
    rank = jnp.sum((jnp.cumsum(hits, axis=-2) - 1) * hits, axis=-1)
    return owners * capacity + rank


def to_blocks(plane):
    nrows, width = plane.shape
    return (
        plane.reshape(nrows // BLOCK_ROWS, BLOCK_ROWS, width // BLOCK_COLUMNS, BLOCK_COLUMNS)
        .transpose(0, 2, 1, 3)
        .reshape(-1, BLOCK_ROWS * BLOCK_COLUMNS)
    )


def from_blocks(blocks, nrows, width):
    return (
        blocks.reshape(nrows // BLOCK_ROWS, width // BLOCK_COLUMNS, BLOCK_ROWS, BLOCK_COLUMNS)
        .transpose(0, 2, 1, 3)
        .reshape(nrows, width)
    )


def per_device(
    visit_image, mask_bits, visit_weight, basis_cols, basis_rows, kernel_coef, row_warp,
    col_warp, dest_owner, dest_block, new_science, tmpl_owner, tmpl_block,
):
    nrows, width = visit_image.shape
    ntile = lax.axis_size("tile")
    nccd = lax.axis_size("ccd")
    me = lax.axis_index("ccd")
    nblocks = nrows // BLOCK_ROWS * (width // BLOCK_COLUMNS)
    capacity = 2 * nblocks // nccd
    nslots = nccd * capacity
    down = [(i, i + 1) for i in range(ntile - 1)]
    up = [(i + 1, i) for i in range(ntile - 1)]
    top = lax.ppermute(visit_image[-HALO:], "tile", down)
    bottom = lax.ppermute(visit_image[:HALO], "tile", up)
    bad = jnp.bitwise_and(mask_bits, 3) == 3
    weight_plane = jnp.where(bad, 0.0, visit_weight[0]).astype(jnp.bfloat16)
    weights = lax.all_gather(weight_plane, "tile", axis=0, tiled=True)
    tables = lax.all_gather(
        jnp.stack([dest_owner[:, 0], dest_block, tmpl_owner[:, 0], tmpl_block]), "ccd", axis=0
    )
    flux = convolve(
        visit_image, top, bottom, mask_bits, visit_weight, kernel_coef[0], basis_cols, basis_rows,
        nrows * ntile,
    )
    fluxes = lax.all_gather(flux, "tile", axis=0, tiled=True)

    def warp(plane):
        rowed = jnp.dot(row_warp, plane, preferred_element_type=jnp.float32).astype(jnp.bfloat16)
        return jnp.dot(rowed, col_warp[0], preferred_element_type=jnp.float32).astype(jnp.bfloat16)

    slots = slot_of(dest_owner[:, 0], nccd, capacity)
    select = (slots[None, :] == jnp.arange(nslots)[:, None]).astype(jnp.bfloat16)
    tslots = slot_of(tmpl_owner[:, 0], nccd, capacity)
    tselect = (tslots[:, None] == jnp.arange(nslots)[None, :]).astype(jnp.bfloat16)

    def arriving(owners, blocks):
        rank = slot_of(owners, nccd, capacity) - owners * capacity
        mine = owners == me
        hit = (rank[:, None, :] == jnp.arange(capacity)[None, :, None]) & mine[:, None, :]
        return jnp.max(jnp.where(hit, blocks[:, None, :], -1), axis=-1).reshape(-1)

    landing = arriving(tables[:, 0], tables[:, 1])
    wanted = arriving(tables[:, 2], tables[:, 3])
    place = (landing[None, :] == jnp.arange(nblocks)[:, None]).astype(jnp.bfloat16)
    serve = (wanted[:, None] == jnp.arange(nblocks)[None, :]).astype(jnp.bfloat16)

    def swap(x):
        x = x.reshape(nccd, capacity, -1)
        y = lax.all_to_all(x, "ccd", split_axis=0, concat_axis=0, tiled=True)
        return y.reshape(nslots, -1)

    def send(plane):
        out = jnp.dot(select, to_blocks(warp(plane)), preferred_element_type=jnp.float32)
        return swap(out.astype(jnp.bfloat16))

    den = jnp.dot(place, send(weights), preferred_element_type=jnp.float32)
    num = jnp.dot(place, send(fluxes), preferred_element_type=jnp.float32)
    coadd_blocks = num / jnp.maximum(den, FLOOR)
    reply = jnp.dot(serve, coadd_blocks.astype(jnp.bfloat16), preferred_element_type=jnp.float32)
    back = swap(reply.astype(jnp.bfloat16))
    template = jnp.dot(tselect, back, preferred_element_type=jnp.float32)
    return (
        from_blocks(coadd_blocks, nrows, width),
        new_science - from_blocks(template, nrows, width),
    )


def solution(mesh):
    both = P(("ccd", "tile"), None)
    flat = P(("ccd", "tile"))
    three = P("ccd", None, None)
    return jax.shard_map(
        per_device,
        mesh=mesh,
        in_specs=(
            both, both, P("ccd"), P(), P(), three, both, three, both, flat, both, both, flat,
        ),
        out_specs=(both, both),
        check_vma=False,
    )
```

```python
import functools

import jax
import jax.numpy as jnp
from jax import lax
from jax.experimental import pallas as pl
from jax.experimental.pallas import tpu as pltpu
from jax.sharding import PartitionSpec as P

BLOCK_ROWS = 16
BLOCK_COLUMNS = 128
FLOOR = 1.0
HALO = 16
SPAN = 256
STEP = 208
GROUP = 4


def conv_kernel(
    ntaps, cutout_rows, coef_ref, weight_ref, top_ref, image_ref, bottom_ref, mask_ref,
    cols_ref, rows_ref, flux_ref, ext_ref, acc_ref,
):
    nrows, width = image_ref.shape
    half = (ntaps - 1) // 2
    nwin = -(-width // STEP)
    nbasis = cols_ref.shape[0]
    left = 128
    ext = jnp.concatenate([top_ref[...], image_ref[...], bottom_ref[...]], axis=0).astype(jnp.float32)
    high = ext.shape[0]
    ext = jnp.concatenate(
        [jnp.zeros((high, left), jnp.float32), ext, jnp.zeros((high, 3 * 128), jnp.float32)], axis=1
    )
    ext_ref[...] = jnp.zeros_like(ext_ref)
    for k in range(nwin):
        start = STEP * k - half + left
        base = start // 128 * 128
        piece = ext[:, base : base + SPAN + 128]
        shift = start - base
        if shift:
            piece = pltpu.roll(piece, SPAN + 128 - shift, 1)
        ext_ref[0:high, k * SPAN : (k + 1) * SPAN] = piece[:, :SPAN].astype(jnp.bfloat16)
    first_row = lax.axis_index("tile") * nrows
    row = (first_row + lax.broadcasted_iota(jnp.int32, (nrows, SPAN), 0)).astype(jnp.float32)
    yn = (2.0 * row + 1.0) / cutout_rows - 1.0
    yy = yn * yn
    lane = lax.broadcasted_iota(jnp.int32, (1, SPAN), 1).astype(jnp.float32)
    acc_ref[...] = jnp.zeros_like(acc_ref)

    def one(b):
        taps = jnp.broadcast_to(cols_ref[pl.ds(b, 1), :], (nrows, SPAN))
        vtab = pltpu.roll(taps, 0, 1, stride=1, stride_axis=0).astype(jnp.bfloat16)
        taps = jnp.broadcast_to(rows_ref[pl.ds(b, 1), :], (SPAN, SPAN))
        htab = pltpu.roll(taps, 0, 1, stride=1, stride_axis=0).astype(jnp.bfloat16)
        vert = jnp.dot(vtab, ext_ref[...], preferred_element_type=jnp.float32).astype(jnp.bfloat16)
        c = [coef_ref[b, p] for p in range(6)]
        yyc = yy * c[3]
        stacked = jnp.concatenate([vert[:, k * SPAN : (k + 1) * SPAN] for k in range(nwin)], axis=0)
        horiz = jnp.dot(stacked, htab, preferred_element_type=jnp.float32)
        out = []
        for k in range(nwin):
            xn = (2.0 * (lane + float(STEP * k)) + 1.0) / width - 1.0
            even = c[0] + xn * (c[2] + xn * c[5])
            slope = c[1] + xn * c[4]
            out.append((yyc + even + yn * slope) * horiz[k * nrows : (k + 1) * nrows])
        return out

    def body(g, carry):
        total = one(g * GROUP)
        for u in range(1, GROUP):
            total = [a + b for a, b in zip(total, one(g * GROUP + u))]
        for k in range(nwin):
            acc_ref[k] += total[k]
        return carry

    lax.fori_loop(0, nbasis // GROUP, body, 0)
    conv = jnp.concatenate([acc_ref[k][:, :STEP] for k in range(nwin)], axis=1)[:, :width]
    bad = jnp.bitwise_and(mask_ref[...], 3) == 3
    plane = jnp.where(bad, 0.0, weight_ref[0]).astype(jnp.bfloat16).astype(jnp.float32)
    flux_ref[...] = (plane * conv).astype(jnp.bfloat16)


def convolve(image, top, bottom, mask, weight, coef, basis_cols, basis_rows, cutout_rows):
    nrows, width = image.shape
    nb, ntaps = basis_cols.shape
    half = (ntaps - 1) // 2
    padb = -nb % GROUP
    nwin = -(-width // STEP)
    cols = jnp.pad(
        basis_cols.astype(jnp.float32),
        ((0, padb), (HALO - half, SPAN - ntaps - (HALO - half))),
    )
    rows = basis_rows.astype(jnp.float32)
    rows = jnp.concatenate(
        [rows[:, :1], jnp.zeros((nb, SPAN - ntaps), jnp.float32), rows[:, :0:-1]], axis=1
    )
    rows = jnp.pad(rows, ((0, padb), (0, 0)))
    coef = jnp.pad(coef, ((0, padb), (0, 0)))
    smem = pl.BlockSpec(memory_space=pltpu.SMEM)
    vmem = pl.BlockSpec(memory_space=pltpu.VMEM)
    return pl.pallas_call(
        functools.partial(conv_kernel, ntaps, cutout_rows),
        out_shape=jax.ShapeDtypeStruct((nrows, width), jnp.bfloat16),
        in_specs=[smem, smem] + [vmem] * 6,
        out_specs=vmem,
        scratch_shapes=[
            pltpu.VMEM((SPAN, nwin * SPAN), jnp.bfloat16),
            pltpu.VMEM((nwin, nrows, SPAN), jnp.float32),
        ],
        compiler_params=pltpu.CompilerParams(vmem_limit_bytes=40 << 20),
        cost_estimate=pl.CostEstimate(flops=10 * 10**9, bytes_accessed=2 << 20, transcendentals=0),
        name="conv_flux",
    )(coef, weight, top, image, bottom, mask, cols, rows)


def slot_of(owners, count, capacity):
    hits = (owners[..., :, None] == jnp.arange(count)).astype(jnp.int32)
    rank = jnp.sum((jnp.cumsum(hits, axis=-2) - 1) * hits, axis=-1)
    return owners * capacity + rank


def from_blocks(blocks, nrows, width):
    return (
        blocks.reshape(nrows // BLOCK_ROWS, width // BLOCK_COLUMNS, BLOCK_ROWS, BLOCK_COLUMNS)
        .transpose(0, 2, 1, 3)
        .reshape(nrows, width)
    )


MESH = pl.DeviceIdType.MESH


def exchange_kernel(
    nccd, source_ref, flux_ref, own_ref, across_ref, row_ref, col_ref, wout_ref, fout_ref,
    planes, blocks, outgoing, arriving, hop_send, hop_recv, send_sem, recv_sem,
):
    nrows, width = flux_ref.shape
    across_columns = width // BLOCK_COLUMNS
    ccd, tile = lax.axis_index("ccd"), lax.axis_index("tile")
    mate = tile + 1 - 2 * lax.rem(tile, 2)
    opposite = lax.rem(tile + 2, 4)
    far = lax.rem(mate + 2, 4)
    barrier = pltpu.get_barrier_semaphore()
    for near in (mate, opposite):
        pl.semaphore_signal(barrier, inc=1, device_id=(ccd, near), device_id_type=MESH)
    for d in range(1, nccd):
        pl.semaphore_signal(
            barrier, inc=1, device_id=(lax.rem(ccd + d, nccd), tile), device_id_type=MESH
        )
    pl.semaphore_wait(barrier, nccd + 1)

    def hop(index, source, slot, target):
        copy = pltpu.make_async_remote_copy(
            src_ref=source, dst_ref=planes.at[slot], send_sem=hop_send.at[index],
            recv_sem=hop_recv.at[index], device_id=(ccd, target), device_id_type=MESH,
        )
        copy.start()
        return copy

    flux_far = hop(0, flux_ref, 1, opposite)
    own_mate = hop(1, own_ref, 2, mate)
    across_mate = hop(2, across_ref, 3, mate)
    flux_mate = hop(3, flux_ref, 0, mate)

    def part(position, plane):
        columns = pl.ds(pl.multiple_of(position * nrows, 128), nrows)
        return jnp.dot(row_ref[:, columns], plane, preferred_element_type=jnp.float32)

    def push(k, own, mates, opposites, fars):
        rowed = part(tile, own) + part(mate, mates) + part(opposite, opposites) + part(far, fars)
        warped = jnp.dot(
            rowed.astype(jnp.bfloat16), col_ref[...], preferred_element_type=jnp.float32
        ).astype(jnp.bfloat16)
        for i in range(nrows // BLOCK_ROWS):
            for j in range(across_columns):
                blocks[k, i * across_columns + j] = warped[
                    i * BLOCK_ROWS : (i + 1) * BLOCK_ROWS,
                    j * BLOCK_COLUMNS : (j + 1) * BLOCK_COLUMNS,
                ]
        capacity = outgoing.shape[2]
        copies = []
        for step in range(nccd):
            d = (step + 1) % nccd
            target = outgoing if d else arriving

            def fill(c, carry):
                target[k, d, c] = blocks[k, source_ref[d * capacity + c]]
                return carry

            lax.fori_loop(0, capacity, fill, 0, unroll=True)
            if d:
                copy = pltpu.make_async_remote_copy(
                    src_ref=outgoing.at[k, d], dst_ref=arriving.at[k, d],
                    send_sem=send_sem.at[k, d], recv_sem=recv_sem.at[k, d],
                    device_id=(lax.rem(ccd + d, nccd), tile), device_id_type=MESH,
                )
                copy.start()
                copies.append(copy)
        return copies

    own_mate.wait()
    across_mate.wait()
    copies = push(0, own_ref[...], planes[2], across_ref[...], planes[3])
    flux_far.wait()
    flux_last = hop(4, planes.at[1], 4, mate)
    flux_mate.wait()
    flux_last.wait()
    copies += push(1, flux_ref[...], planes[0], planes[1], planes[4])
    for copy in copies[: nccd - 1]:
        copy.wait()
    wout_ref[...] = arriving[0]
    for copy in copies[nccd - 1 :]:
        copy.wait()
    fout_ref[...] = arriving[1]


def exchange(source, flux, own, across, row_warp, col_warp, nccd, capacity):
    nrows, width = flux.shape
    nblocks = nrows // BLOCK_ROWS * (width // BLOCK_COLUMNS)
    shape = (nccd, capacity, BLOCK_ROWS, BLOCK_COLUMNS)
    vmem = pl.BlockSpec(memory_space=pltpu.VMEM)
    return pl.pallas_call(
        functools.partial(exchange_kernel, nccd),
        out_shape=[jax.ShapeDtypeStruct(shape, jnp.bfloat16)] * 2,
        in_specs=[pl.BlockSpec(memory_space=pltpu.SMEM)] + [vmem] * 5,
        out_specs=[vmem, vmem],
        scratch_shapes=[
            pltpu.VMEM((5, nrows, width), jnp.bfloat16),
            pltpu.VMEM((2, nblocks, BLOCK_ROWS, BLOCK_COLUMNS), jnp.bfloat16),
            pltpu.VMEM((2,) + shape, jnp.bfloat16),
            pltpu.VMEM((2,) + shape, jnp.bfloat16),
            pltpu.SemaphoreType.DMA((5,)),
            pltpu.SemaphoreType.DMA((5,)),
            pltpu.SemaphoreType.DMA((2, nccd)),
            pltpu.SemaphoreType.DMA((2, nccd)),
        ],
        compiler_params=pltpu.CompilerParams(
            vmem_limit_bytes=40 << 20, collective_id=0, has_side_effects=True
        ),
        cost_estimate=pl.CostEstimate(flops=10**9, bytes_accessed=6 << 20, transcendentals=0),
        name="gather_warp_exchange",
    )(source, flux, own, across, row_warp, col_warp)


def per_device(
    visit_image, mask_bits, visit_weight, basis_cols, basis_rows, kernel_coef, row_warp,
    col_warp, dest_owner, dest_block, new_science, tmpl_owner, tmpl_block,
):
    nrows, width = visit_image.shape
    ntile = lax.axis_size("tile")
    nccd = lax.axis_size("ccd")
    me = lax.axis_index("ccd")
    nblocks = nrows // BLOCK_ROWS * (width // BLOCK_COLUMNS)
    capacity = 2 * nblocks // nccd
    nslots = nccd * capacity
    down = [(i, i + 1) for i in range(ntile - 1)]
    up = [(i + 1, i) for i in range(ntile - 1)]
    top = lax.ppermute(visit_image[-HALO:], "tile", down)
    bottom = lax.ppermute(visit_image[:HALO], "tile", up)
    bad = jnp.bitwise_and(mask_bits, 3) == 3
    weight_plane = jnp.where(bad, 0.0, visit_weight[0]).astype(jnp.bfloat16)
    across = lax.ppermute(weight_plane, "tile", [(i, (i + 2) % ntile) for i in range(ntile)])
    tables = lax.all_gather(
        jnp.stack([dest_owner[:, 0], dest_block, tmpl_owner[:, 0], tmpl_block]), "ccd", axis=0
    )
    flux = convolve(
        visit_image, top, bottom, mask_bits, visit_weight, kernel_coef[0], basis_cols, basis_rows,
        nrows * ntile,
    )
    slots = slot_of(dest_owner[:, 0], nccd, capacity)
    order = jnp.arange(nccd)
    target_slots = ((me + order) % nccd)[:, None] * capacity + jnp.arange(capacity)[None, :]
    select = slots[None, :] == target_slots.reshape(-1)[:, None]
    source = jnp.sum(jnp.where(select, jnp.arange(nblocks)[None, :], 0), axis=1).astype(jnp.int32)
    tslots = slot_of(tmpl_owner[:, 0], nccd, capacity)
    tselect = (tslots[:, None] == jnp.arange(nslots)[None, :]).astype(jnp.bfloat16)

    def arriving(owners, blocks):
        rank = slot_of(owners, nccd, capacity) - owners * capacity
        mine = owners == me
        hit = (rank[:, None, :] == jnp.arange(capacity)[None, :, None]) & mine[:, None, :]
        return jnp.max(jnp.where(hit, blocks[:, None, :], -1), axis=-1)

    landing = jnp.take(arriving(tables[:, 0], tables[:, 1]), (me - order) % nccd, axis=0)
    landing = landing.reshape(-1)
    wanted = arriving(tables[:, 2], tables[:, 3]).reshape(-1)
    place = (landing[None, :] == jnp.arange(nblocks)[:, None]).astype(jnp.bfloat16)
    serve = (wanted[:, None] == jnp.arange(nblocks)[None, :]).astype(jnp.bfloat16)

    def swap(x):
        x = x.reshape(nccd, capacity, -1)
        y = lax.all_to_all(x, "ccd", split_axis=0, concat_axis=0, tiled=True)
        return y.reshape(nslots, -1)

    arrived = exchange(
        source, flux, weight_plane, across, row_warp, col_warp[0], nccd, capacity
    )
    den, num = (
        jnp.dot(place, x.reshape(nslots, -1), preferred_element_type=jnp.float32) for x in arrived
    )
    coadd_blocks = num / jnp.maximum(den, FLOOR)
    reply = jnp.dot(serve, coadd_blocks.astype(jnp.bfloat16), preferred_element_type=jnp.float32)
    back = swap(reply.astype(jnp.bfloat16))
    template = jnp.dot(tselect, back, preferred_element_type=jnp.float32)
    return (
        from_blocks(coadd_blocks, nrows, width),
        new_science - from_blocks(template, nrows, width),
    )


def solution(mesh):
    both = P(("ccd", "tile"), None)
    flat = P(("ccd", "tile"))
    three = P("ccd", None, None)
    return jax.shard_map(
        per_device,
        mesh=mesh,
        in_specs=(
            both, both, P("ccd"), P(), P(), three, both, three, both, flat, both, both, flat,
        ),
        out_specs=(both, both),
        check_vma=False,
    )
```
